768 devices in a mesh: outer: 96 (over x, y, z_hi), inner: 8 (over z_lo, core).
Axes of the slice: x: 4, y: 8, z: 12 (z_hi: 3, z_lo: 4; z = z_hi * 4 + z_lo), core: 2. Of those that a mesh axis runs over, the one named last changes fastest.
Arguments:
- x_normed: bfloat16 [393216, 3840], P(('outer', 'inner')), may hold values from -24 to 24
- key_grad: bfloat16 [393216, 128], P(('outer', 'inner')), may hold values from -0.009765625 to 0.009765625
- value_grad: bfloat16 [393216, 128], P(('outer', 'inner')), may hold values from -0.009765625 to 0.009765625
Outputs:
- key_weight_grad: float32 [3840, 128], P(('outer', 'inner'))
- value_weight_grad: float32 [3840, 128], P(('outer', 'inner'))
The draws below stay inside these ranges and needn't reach their ends.
All inputs are finite; a program needn't handle non-finite values.
Results may differ from the reference program's by a relative error of at most 0.0029.
Values may be sent and summed in bfloat16 or wider, within the bound.
A program may use at most 32 MiB of HBM per device.

```python
import jax
import jax.numpy as jnp
from jax import lax

D_WIN = 3840
HEAD = 128
TOK_DEV = 512
TOKENS = 393216
N_OUTER = 96
N_INNER = 8


def raised(values, key, source, target, blocks, factor):
    owner, partner = [(jnp.arange(values.shape[axis_at]) // (values.shape[axis_at] // blocks)).reshape([-1 if axis == axis_at else 1 for axis in range(values.ndim)]) for axis_at in (source, target)]
    chosen = jax.random.permutation(key, blocks)[partner]
    strong = (owner == chosen) | (owner == (partner + blocks // 2) % blocks)
    return jnp.where(strong, factor * values, values)


def block_scale(own_key, shape, shards, smallest, high):
    def one(position, parts):
        heights = jax.random.uniform(jax.random.fold_in(jax.random.fold_in(own_key, 6), position), (parts,), jnp.float32, smallest / len(shards), high / len(shards))
        return jnp.repeat(jnp.exp(heights), shape[position] // parts).reshape((-1,) + (1,) * (len(shape) - position - 1))

    loudness = one(*shards[0])
    for cut in shards[1:]:
        loudness = loudness * one(*cut)
    return loudness


def normal_values(stream_key, dims, spread, most, split=(), held_as=jnp.bfloat16):
    loudness = block_scale(stream_key, dims, split, -0.22, 0.18) if split else 1.0
    entries = jax.random.normal(stream_key, dims, jnp.float32) * spread * loudness
    return jnp.minimum(jnp.maximum(entries, -most), most).astype(held_as)


def heavy_noise(stream_key, extent, spread, limit, cuts, heavy, held_as=jnp.bfloat16):
    array = spread * jax.random.normal(stream_key, extent, jnp.float32)
    if cuts:
        array = array * block_scale(stream_key, extent, cuts, -0.22, 0.18)
    return jnp.clip(raised(array, jax.random.fold_in(stream_key, 3), *heavy), -limit, limit).astype(held_as)


def setup_inputs(seed: int = 0) -> dict:
    seeds = jax.random.split(jax.random.key(seed), 4)
    x_normed = heavy_noise(seeds[0], (TOKENS, D_WIN), 1.0, 24.0, ((0, 768),), (0, 1, 768, 6.0))
    key_grad = normal_values(seeds[1], (TOKENS, HEAD), TOKENS ** -0.5, 0.009765625, ((0, 768),))
    value_grad = normal_values(seeds[2], (TOKENS, HEAD), TOKENS ** -0.5, 0.009765625, ((0, 768),))
    return {"x_normed": x_normed, "key_grad": key_grad, "value_grad": value_grad}


def reference(x_normed, key_grad, value_grad):
    inputs = x_normed.reshape(N_OUTER, N_INNER, TOK_DEV, D_WIN)
    key_blocks = key_grad.reshape(N_OUTER, N_INNER, TOK_DEV, HEAD)
    value_blocks = value_grad.reshape(N_OUTER, N_INNER, TOK_DEV, HEAD)

    def group_step(carry, pieces):
        group_x, group_k, group_v = pieces
        wide = group_x.astype(jnp.float32)
        results = []
        for cotangent, total in ((group_k, carry[0]), (group_v, carry[1])):
            partial_value = jnp.einsum("jtd,jth->jdh", wide, cotangent.astype(jnp.float32))
            rounded = lax.optimization_barrier(partial_value.astype(jnp.bfloat16))
            results.append(total + jnp.sum(rounded.astype(jnp.float32), axis=0))
        return (results[0], results[1]), None

    start = jnp.zeros((D_WIN, HEAD), jnp.float32)
    (key_total, value_total), _ = lax.scan(group_step, (start, start), (inputs, key_blocks, value_blocks))
    return key_total, value_total
```

```python
import jax
import jax.numpy as jnp
from jax import lax
from jax.experimental import pallas as pl
from jax.experimental.pallas import tpu as pltpu
from jax.sharding import PartitionSpec as P

MESH = pl.DeviceIdType.MESH
NX, NY, NZ = 4, 8, 12
D_WIN, HEAD, TOK = 3840, 128, 512
PAIR = 240
ROWS = 120
PAD = 128
OWN = 5
LOAD = 768
COLS = 256
bf16, f32 = jnp.bfloat16, jnp.float32


def device(x, y, z, core):
    return ((x * NY + y) * 3 + z // 4, (z % 4) * 2 + core)


def kernel(
    x_hbm, k_hbm, v_hbm, out, xv, g, give, keep, got, xs, xr, ysum, ys, yr, total, zs, zr,
    load_sem, core_send, core_recv, x_send, x_recv, y_send, y_recv, z_send, z_recv,
):
    outer, inner = lax.axis_index("outer"), lax.axis_index("inner")
    x, y = outer // (NY * 3), (outer // 3) % NY
    z, core = (outer % 3) * 4 + inner // 2, inner % 2
    other = 1 - core

    loads = [pltpu.make_async_copy(k_hbm, g.at[0], load_sem.at[0]), pltpu.make_async_copy(v_hbm, g.at[1], load_sem.at[1])]
    for n in range(D_WIN // LOAD):
        part = pl.ds(n * LOAD, LOAD)
        loads.append(pltpu.make_async_copy(x_hbm.at[:, part], xv.at[:, part], load_sem.at[2 + n]))
    for copy in loads:
        copy.start()

    peers = [device(x, y, z, other)]
    peers += [device((x + d) % NX, y, z, core) for d in range(1, NX)]
    peers += [device(x, (y + d) % NY, z, core) for d in range(1, NY)]
    peers += [device(x, y, (z + d) % NZ, c) for d in range(1, NZ) for c in range(2)]
    barrier = pltpu.get_barrier_semaphore()
    for peer in peers:
        pl.semaphore_signal(barrier, inc=1, device_id=peer, device_id_type=MESH)

    loads[0].wait()
    loads[1].wait()
    gt = jnp.concatenate([g[other].T, g[core].T], axis=0)
    for n in range(D_WIN // COLS):
        if n % (LOAD // COLS) == 0:
            loads[2 + n // (LOAD // COLS)].wait()
        part = jnp.dot(gt, xv[:, n * COLS : (n + 1) * COLS], preferred_element_type=f32).astype(bf16)
        for half, dest in ((part[:HEAD].T, give), (part[HEAD:].T, keep)):
            at = n * COLS
            while at < (n + 1) * COLS:
                end = min((at // PAIR + 1) * PAIR, (n + 1) * COLS)
                pair, lo = at // PAIR, at % PAIR
                dest[pair // 4, pair % 4, lo : lo + end - at, :] = half[at - n * COLS : end - n * COLS]
                at = end
    pl.semaphore_wait(barrier, len(peers))

    def remote(src, dst, send, recv, to):
        return pltpu.make_async_remote_copy(
            src_ref=src, dst_ref=dst, send_sem=send, recv_sem=recv, device_id=to, device_id_type=MESH
        )

    mine = y // 2
    order = [(mine + d) % 4 for d in (2, 1, 3, 0)]
    swaps = []
    for p, q in enumerate(order):
        swaps.append(remote(give.at[:, q], got.at[p], core_send.at[p], core_recv.at[p], peers[0]))
        swaps[p].start()

    sent = []

    def along_x(p):
        swaps[p].wait_recv()
        q = order[p]
        for n in range(NX):
            xs[p, n] = (keep[n, q].astype(f32) + got[p, n].astype(f32)).astype(bf16)
        for d in (2, 1, 3):
            to = (x + d) % NX
            copy = remote(xs.at[p, to], xr.at[p, d - 1], x_send.at[p, d - 1], x_recv.at[p], device(to, y, z, core))
            copy.start()
            sent.append(copy)

    def along_y(p):
        pltpu.make_async_copy(xr.at[p], xr.at[p], x_recv.at[p]).wait()
        s = xs[p, x].astype(f32)
        for d in range(NX - 1):
            s += xr[p, d].astype(f32)
        if p < 3:
            for j in range(2):
                ys[p, j, :ROWS] = s[j * ROWS : (j + 1) * ROWS].astype(bf16)
            for j in range(2):
                to = order[p] * 2 + j
                copy = remote(
                    ys.at[p, j], yr.at[(y - to + NY) % NY - 1], y_send.at[p, j], y_recv, device(x, to, z, core)
                )
                copy.start()
                sent.append(copy)
        else:
            for j in range(2):
                ysum[j] = s[j * ROWS : (j + 1) * ROWS]
            own, j = y % 2, 1 - y % 2
            ys[p, 0, :ROWS] = ysum[j].astype(bf16)
            to = order[p] * 2 + j
            copy = remote(
                ys.at[p, 0], yr.at[(y - to + NY) % NY - 1], y_send.at[p, 0], y_recv, device(x, to, z, core)
            )
            copy.start()
            sent.append(copy)

    for p in range(4):
        along_x(p)
        if p >= 1:
            along_y(p - 1)
    along_y(3)

    pltpu.make_async_copy(yr, yr, y_recv).wait()
    s = ysum[y % 2]
    for d in range(NY - 1):
        s += yr[d, :ROWS].astype(f32)
    total[...] = s
    for n in range(2 * NZ):
        zs[n, :OWN] = total[n * OWN : (n + 1) * OWN]
    for d in (6, 5, 7, 4, 8, 3, 9, 2, 10, 1, 11, 0):
        to = (z + d) % NZ
        for c in (0, 1) if d else (0,):
            c = c if d else other
            copy = remote(
                zs.at[to * 2 + c, pl.ds(0, OWN)],
                zr.at[core * NZ + d, pl.ds(0, OWN)],
                z_send.at[d * 2 + (c if d else 0)],
                z_recv,
                device(x, y, to, c),
            )
            copy.start()
            sent.append(copy)
    zr[core * NZ, :OWN] = zs[z * 2 + core, :OWN]
    got_all = zr.at[pl.ds(0, 2 * NZ - 1), pl.ds(0, OWN)]
    pltpu.make_async_copy(got_all, got_all, z_recv).wait()
    for t in range(2):
        s = zr[t * NZ, :OWN]
        for d in range(1, NZ):
            s += zr[t * NZ + d, :OWN]
        out[t, :OWN] = s
    for copy in swaps + sent:
        copy.wait_send()


def split(both, key_out, value_out):
    key_out[...] = both[0, :OWN]
    value_out[...] = both[1, :OWN]


def per_device(x_normed, key_grad, value_grad):
    hbm = pl.BlockSpec(memory_space=pl.ANY)
    vmem = pl.BlockSpec(memory_space=pltpu.VMEM)
    dma = pltpu.SemaphoreType.DMA
    both = pl.pallas_call(
        kernel,
        out_shape=jax.ShapeDtypeStruct((2, 8, HEAD), f32),
        in_specs=[hbm] * 3,
        out_specs=vmem,
        scratch_shapes=[
            pltpu.VMEM((TOK, D_WIN), bf16),
            pltpu.VMEM((2, TOK, HEAD), bf16),
            pltpu.VMEM((NX, 4, PAIR, HEAD), bf16),
            pltpu.VMEM((NX, 4, PAIR, HEAD), bf16),
            pltpu.VMEM((4, NX, PAIR, HEAD), bf16),
            pltpu.VMEM((4, NX, PAIR, HEAD), bf16),
            pltpu.VMEM((4, NX - 1, PAIR, HEAD), bf16),
            pltpu.VMEM((2, ROWS, HEAD), f32),
            pltpu.VMEM((4, 2, PAD, HEAD), bf16),
            pltpu.VMEM((NY - 1, PAD, HEAD), bf16),
            pltpu.VMEM((ROWS, HEAD), f32),
            pltpu.VMEM((2 * NZ, 8, HEAD), f32),
            pltpu.VMEM((2 * NZ, 8, HEAD), f32),
            dma((2 + D_WIN // LOAD,)),
            dma((4,)),
            dma((4,)),
            dma((4, NX - 1)),
            dma((4,)),
            dma((4, 2)),
            dma,
            dma((2 * NZ,)),
            dma,
        ],
        compiler_params=pltpu.CompilerParams(
            collective_id=0, has_side_effects=True, vmem_limit_bytes=60 * 1024 * 1024
        ),
    )(x_normed, key_grad, value_grad)
    owned = jax.ShapeDtypeStruct((OWN, HEAD), f32)
    return pl.pallas_call(split, out_shape=(owned, owned), in_specs=[vmem], out_specs=(vmem, vmem))(both)


def solution(mesh):
    rows = P(("outer", "inner"), None)
    return jax.shard_map(per_device, mesh=mesh, in_specs=(rows,) * 3, out_specs=(rows, rows), check_vma=False)
```

```python
import jax
import jax.numpy as jnp
from jax import lax
from jax.experimental import pallas as pl
from jax.experimental.pallas import tpu as pltpu
from jax.sharding import PartitionSpec as P

MESH = pl.DeviceIdType.MESH
NX, NY, NZ = 4, 8, 12
D_WIN, HEAD, TOK = 3840, 128, 512
ROWS = 120
OWN = 5
LOAD = 768
COLS = 256
PIECES = ((0, 16), (16, 32), (32, 64), (64, 96), (96, 120))
HEIGHTS = tuple(-(-(hi - lo) // 16) * 16 for lo, hi in PIECES)
ORDER = ("x0", "x1", "x2", "x3", "x4", "y0", "y1", "y2", "z0", "z1", "y3", "z2", "y4", "z3", "z4")
bf16, f32 = jnp.bfloat16, jnp.float32


def device(x, y, z, core):
    return ((x * NY + y) * 3 + z // 4, (z % 4) * 2 + core)


def kernel(x_hbm, k_hbm, v_hbm, out, xv, g, give, keep, got, xs, xr, yf, ys, yr, total, zs, zr, load_sem, core_send,
           core_recv, x_send, x_recv, y_send, y_recv, z_send, z_recv, plane_in, line_in):
    outer, inner = lax.axis_index("outer"), lax.axis_index("inner")
    x, y = outer // (NY * 3), (outer // 3) % NY
    z, core = (outer % 3) * 4 + inner // 2, inner % 2
    other = 1 - core

    loads = [pltpu.make_async_copy(k_hbm, g.at[0], load_sem.at[0]), pltpu.make_async_copy(v_hbm, g.at[1], load_sem.at[1])]
    for n in range(D_WIN // LOAD):
        part = pl.ds(n * LOAD, LOAD)
        loads.append(pltpu.make_async_copy(x_hbm.at[:, part], xv.at[:, part], load_sem.at[2 + n]))
    for copy in loads:
        copy.start()

    barrier = pltpu.get_barrier_semaphore()

    def signal(sem, to):
        pl.semaphore_signal(sem, inc=1, device_id=to, device_id_type=MESH)

    for d in (4, 3, 5, 2, 6, 1, 7):
        signal(barrier, device(x, (y + d) % NY, z, 0))
    for d in (2, 1, 3):
        signal(barrier, device((x + d) % NX, y, z, 0))

    @pl.when(core == 1)
    def _():
        signal(barrier, device(x, y, z, 0))

    for d in (6, 5, 7, 4, 8, 3, 9, 2, 10, 1, 11):
        signal(barrier, device(x, y, (z + d) % NZ, 1))

    loads[0].wait()
    loads[1].wait()
    gt = jnp.concatenate([g[other].T, g[core].T], axis=0)
    for n in range(D_WIN // COLS):
        if n % (LOAD // COLS) == 0:
            loads[2 + n // (LOAD // COLS)].wait()
        start, stop = n * COLS, (n + 1) * COLS
        part = jnp.dot(gt, xv[:, start:stop], preferred_element_type=f32).astype(bf16)
        for half, dest in ((part[:HEAD].T, give), (part[HEAD:].T, keep)):
            for block in range(start // ROWS, -(-stop // ROWS)):
                for p, (lo, hi) in enumerate(PIECES):
                    first, last = max(start, block * ROWS + lo), min(stop, block * ROWS + hi)
                    if first < last:
                        at = first - block * ROWS - lo
                        dest[p][block // NY, block % NY, at : at + last - first, :] = half[first - start : last - start]

    @pl.when(core == 0)
    def _():
        pl.semaphore_wait(barrier, 2 * (NX - 1) + 2 * (NY - 1) + 1)
        signal(plane_in, device(x, y, z, 1))

    @pl.when(core == 1)
    def _():
        pl.semaphore_wait(plane_in, 1)

    def remote(src, dst, send, recv, to):
        return pltpu.make_async_remote_copy(
            src_ref=src, dst_ref=dst, send_sem=send, recv_sem=recv, device_id=to, device_id_type=MESH
        )

    def wait(ref, sem):
        pltpu.make_async_copy(ref, ref, sem).wait()

    swaps = [
        remote(give[p], got[p], core_send.at[p], core_recv.at[p], device(x, y, z, other)) for p in range(len(PIECES))
    ]
    for swap in swaps:
        swap.start()

    def along_x(p):
        swaps[p].wait_recv()
        for n in range(NX):
            xs[p][n] = (keep[p][n].astype(f32) + got[p][n].astype(f32)).astype(bf16)
        for d in (2, 1, 3):
            to = (x + d) % NX
            remote(xs[p].at[to], xr[p].at[d - 1], x_send.at[p], x_recv.at[p], device(to, y, z, core)).start()

    def along_y(p):
        wait(xr[p], x_recv.at[p])
        s = keep[p][x].astype(f32) + got[p][x].astype(f32)
        for d in range(NX - 1):
            s += xr[p][d].astype(f32)
        yf[p][...] = s
        ys[p][...] = s.astype(bf16)
        for d in (4, 3, 5, 2, 6, 1, 7):
            to = (y + d) % NY
            remote(ys[p].at[to], yr[p].at[d - 1], y_send.at[p], y_recv.at[p], device(x, to, z, core)).start()

    def along_z(p):
        wait(yr[p], y_recv.at[p])
        s = yf[p][y]
        for d in range(NY - 1):
            s += yr[p][d].astype(f32)
        lo, hi = PIECES[p]
        total[lo : lo + HEIGHTS[p]] = s
        for to in range(NZ):
            if not lo < (to + 1) * 2 * OWN <= hi:
                continue
            for c in range(2):
                n = to * 2 + c
                zs[n, :OWN] = total[n * OWN : (n + 1) * OWN]

                @pl.when(jnp.logical_or(z != to, core != c))
                def _():
                    src, dst = zs.at[n, pl.ds(0, OWN)], zr.at[core * NZ + z, pl.ds(0, OWN)]
                    remote(src, dst, z_send, z_recv, device(x, y, to, c)).start()

    def meet_z():
        @pl.when(core == 1)
        def _():
            pl.semaphore_wait(barrier, 2 * (NZ - 1))
            signal(line_in, device(x, y, z, 0))

        @pl.when(core == 0)
        def _():
            pl.semaphore_wait(line_in, 1)

    steps = {"x": along_x, "y": along_y, "z": along_z}
    for step in ORDER:
        if step == "z0":
            meet_z()
        steps[step[0]](int(step[1]))

    zr[core * NZ + z, :OWN] = zs[z * 2 + core, :OWN]
    for p in range(len(PIECES)):
        swaps[p].wait_send()
        wait(xr[p], x_send.at[p])
        wait(yr[p], y_send.at[p])
    all_but_one = zr.at[pl.ds(0, 2 * NZ - 1), pl.ds(0, OWN)]
    wait(all_but_one, z_send)
    wait(all_but_one, z_recv)
    for t in range(2):
        s = zr[t * NZ, :OWN]
        for d in range(1, NZ):
            s += zr[t * NZ + d, :OWN]
        out[t, :OWN] = s


def split(both, key_out, value_out):
    key_out[...] = both[0, :OWN]
    value_out[...] = both[1, :OWN]


def per_device(x_normed, key_grad, value_grad):
    hbm = pl.BlockSpec(memory_space=pl.ANY)
    vmem = pl.BlockSpec(memory_space=pltpu.VMEM)
    dma = pltpu.SemaphoreType.DMA
    count = len(PIECES)

    def buffers(*dims, dtype=bf16):
        return [pltpu.VMEM((*dims, height, HEAD), dtype) for height in HEIGHTS]

    both = pl.pallas_call(
        kernel,
        out_shape=jax.ShapeDtypeStruct((2, 8, HEAD), f32),
        in_specs=[hbm] * 3,
        out_specs=vmem,
        scratch_shapes=[
            pltpu.VMEM((TOK, D_WIN), bf16),
            pltpu.VMEM((2, TOK, HEAD), bf16),
            buffers(NX, NY),
            buffers(NX, NY),
            buffers(NX, NY),
            buffers(NX, NY),
            buffers(NX - 1, NY),
            buffers(NY, dtype=f32),
            buffers(NY),
            buffers(NY - 1),
            pltpu.VMEM((128, HEAD), f32),
            pltpu.VMEM((2 * NZ, 8, HEAD), f32),
            pltpu.VMEM((2 * NZ, 8, HEAD), f32),
            dma((2 + D_WIN // LOAD,)),
            dma((count,)),
            dma((count,)),
            dma((count,)),
            dma((count,)),
            dma((count,)),
            dma((count,)),
            dma,
            dma,
            pltpu.SemaphoreType.REGULAR,
            pltpu.SemaphoreType.REGULAR,
        ],
        compiler_params=pltpu.CompilerParams(
            collective_id=0, has_side_effects=True, vmem_limit_bytes=60 * 1024 * 1024
        ),
    )(x_normed, key_grad, value_grad)
    owned = jax.ShapeDtypeStruct((OWN, HEAD), f32)
    return pl.pallas_call(split, out_shape=(owned, owned), in_specs=[vmem], out_specs=(vmem, vmem))(both)


def solution(mesh):
    rows = P(("outer", "inner"), None)
    return jax.shard_map(per_device, mesh=mesh, in_specs=(rows,) * 3, out_specs=(rows, rows), check_vma=False)
```

```python
import jax
import jax.numpy as jnp
from jax import lax
from jax.experimental import pallas as pl
from jax.experimental.pallas import tpu as pltpu
from jax.sharding import PartitionSpec as P

MESH = pl.DeviceIdType.MESH
NX, NY, NZ = 4, 8, 12
D_WIN, HEAD, TOK = 3840, 128, 512
ROWS = 120
OWN = 5
LOADS = (2560, 1280)
COLS = 256
PIECES = (
    (0, 0, 16), (0, 16, 32), (1, 0, 16), (0, 32, 48), (1, 16, 32), (0, 48, 64), (1, 32, 64), (0, 64, 96), (1, 64, 80), (0, 96, 120), (1, 80, 120),
)
HEIGHTS = tuple(-(-(hi - lo) // 16) * 16 for _, lo, hi in PIECES)
GROUP = 4
ORDER = (
    "c0", "c1", "x0", "c2", "x1", "c3", "x2", "c4", "x3", "c5", "x4", "c6", "x5", "c7", "x6", "c8", "x7", "y0",
    "c9", "x8", "c10", "x9", "y1", "x10", "y2", "y3", "m0", "y4", "y5", "m1", "z0", "y6", "z1", "z2", "y7",
    "z3", "z4", "z5", "y8", "z6", "y9", "z7", "z8", "y10", "z9", "z10",
)
bf16, f32 = jnp.bfloat16, jnp.float32


def device(x, y, z, core):
    return ((x * NY + y) * 3 + z // 4, (z % 4) * 2 + core)


def kernel(x_hbm, k_hbm, v_hbm, out, xv, g, give, keep, got, xs, xr, yf, ys, yr, total, zs, zr, load_sem, core_send,
           core_recv, x_send, x_recv, y_send, y_recv, z_send, z_recv, plane_in, line_in):
    outer, inner = lax.axis_index("outer"), lax.axis_index("inner")
    x, y = outer // (NY * 3), (outer // 3) % NY
    z, core = (outer % 3) * 4 + inner // 2, inner % 2
    other = 1 - core

    loads = [pltpu.make_async_copy(k_hbm, g.at[0], load_sem.at[0]), pltpu.make_async_copy(v_hbm, g.at[1], load_sem.at[1])]
    segments, at = [], 0
    for n, width in enumerate(LOADS):
        segments.append((at, at + width))
        part = pl.ds(at, width)
        loads.append(pltpu.make_async_copy(x_hbm.at[:, part], xv.at[:, part], load_sem.at[2 + n]))
        at += width
    for copy in loads:
        copy.start()

    barrier = pltpu.get_barrier_semaphore()

    def signal(sem, to):
        pl.semaphore_signal(sem, inc=1, device_id=to, device_id_type=MESH)

    for d in (4, 3, 5, 2, 6, 1, 7):
        signal(barrier, device(x, (y + d) % NY, z, 0))
    for d in (2, 1, 3):
        signal(barrier, device((x + d) % NX, y, z, 0))

    @pl.when(core == 1)
    def _():
        signal(barrier, device(x, y, z, 0))

    for d in (6, 5, 7, 4, 8, 3, 9, 2, 10, 1, 11):
        signal(barrier, device(x, y, (z + d) % NZ, 1))

    def meet_plane():
        @pl.when(core == 0)
        def _():
            pl.semaphore_wait(barrier, 2 * (NX - 1) + 2 * (NY - 1) + 1)
            signal(plane_in, device(x, y, z, 1))

    loads[0].wait()
    loads[1].wait()
    gt = jnp.concatenate([g[other].T, g[core].T], axis=0)
    for n in range(D_WIN // COLS):
        start, stop = n * COLS, (n + 1) * COLS
        for m, (first, last) in enumerate(segments):
            if start == first:
                if m == len(segments) - 1:
                    meet_plane()
                loads[2 + m].wait()
        part = jnp.dot(gt, xv[:, start:stop], preferred_element_type=f32).astype(bf16)
        for half, dest in ((part[:HEAD].T, give), (part[HEAD:].T, keep)):
            for block in range(start // ROWS, -(-stop // ROWS)):
                for p, (group, lo, hi) in enumerate(PIECES):
                    first, last = max(start, block * ROWS + lo), min(stop, block * ROWS + hi)
                    if first < last and block % NY // GROUP == group:
                        at = first - block * ROWS - lo
                        dest[p][block // NY, block % GROUP, at : at + last - first, :] = half[first - start : last - start]


    @pl.when(core == 1)
    def _():
        pl.semaphore_wait(plane_in, 1)

    def remote(src, dst, send, recv, to):
        return pltpu.make_async_remote_copy(
            src_ref=src, dst_ref=dst, send_sem=send, recv_sem=recv, device_id=to, device_id_type=MESH
        )

    def wait(ref, sem):
        pltpu.make_async_copy(ref, ref, sem).wait()

    swaps = [
        remote(give[p], got[p], core_send.at[p], core_recv.at[p], device(x, y, z, other)) for p in range(len(PIECES))
    ]

    def swap_cores(p):
        swaps[p].start()

    def along_x(p):
        swaps[p].wait_recv()
        for n in range(NX):
            xs[p][n] = (keep[p][n].astype(f32) + got[p][n].astype(f32)).astype(bf16)
        for d in (2, 1, 3):
            to = (x + d) % NX
            remote(xs[p].at[to], xr[p].at[d - 1], x_send.at[p], x_recv.at[p], device(to, y, z, core)).start()

    def along_y(p):
        wait(xr[p], x_recv.at[p])
        s = keep[p][x].astype(f32) + got[p][x].astype(f32)
        for d in range(NX - 1):
            s += xr[p][d].astype(f32)
        yf[p][...] = s
        ys[p][...] = s.astype(bf16)
        for n in range(GROUP):
            to = PIECES[p][0] * GROUP + n

            @pl.when(y != to)
            def _():
                slot = (y - to + NY) % NY - 1
                remote(ys[p].at[n], yr[p].at[slot], y_send.at[p], y_recv.at[p], device(x, to, z, core)).start()

    def along_z(p):
        @pl.when(y // GROUP == PIECES[p][0])
        def _():
            wait(yr[p], y_recv.at[p])
            s = yf[p][y % GROUP]
            for d in range(NY - 1):
                s += yr[p][d].astype(f32)
            _, lo, hi = PIECES[p]
            total[lo : lo + HEIGHTS[p]] = s
            for to in range(NZ):
                if not lo < (to + 1) * 2 * OWN <= hi:
                    continue
                for c in range(2):
                    n = to * 2 + c
                    zs[n, :OWN] = total[n * OWN : (n + 1) * OWN]

                    @pl.when(jnp.logical_or(z != to, core != c))
                    def _():
                        src, dst = zs.at[n, pl.ds(0, OWN)], zr.at[core * NZ + z, pl.ds(0, OWN)]
                        remote(src, dst, z_send, z_recv, device(x, y, to, c)).start()

    def meet_line(p):
        if p == 0:

            @pl.when(core == 1)
            def _():
                pl.semaphore_wait(barrier, 2 * (NZ - 1))
                signal(line_in, device(x, y, z, 0))

        else:

            @pl.when(core == 0)
            def _():
                pl.semaphore_wait(line_in, 1)

    steps = {"c": swap_cores, "x": along_x, "y": along_y, "z": along_z, "m": meet_line}
    for step in ORDER:
        steps[step[0]](int(step[1:]))

    zr[core * NZ + z, :OWN] = zs[z * 2 + core, :OWN]
    for p in range(len(PIECES)):
        swaps[p].wait_send()
        wait(xr[p], x_send.at[p])
        wait(yr[p].at[pl.ds(0, GROUP - 1)], y_send.at[p])

        @pl.when(y // GROUP != PIECES[p][0])
        def _():
            wait(yr[p].at[0], y_send.at[p])

    all_but_one = zr.at[pl.ds(0, 2 * NZ - 1), pl.ds(0, OWN)]
    wait(all_but_one, z_send)
    wait(all_but_one, z_recv)
    for t in range(2):
        s = zr[t * NZ, :OWN]
        for d in range(1, NZ):
            s += zr[t * NZ + d, :OWN]
        out[t, :OWN] = s


def per_device(x_normed, key_grad, value_grad):
    hbm = pl.BlockSpec(memory_space=pl.ANY)
    vmem = pl.BlockSpec(memory_space=pltpu.VMEM)
    dma = pltpu.SemaphoreType.DMA
    count = len(PIECES)

    def buffers(*dims, dtype=bf16):
        return [pltpu.VMEM((*dims, height, HEAD), dtype) for height in HEIGHTS]

    both = pl.pallas_call(
        kernel,
        out_shape=jax.ShapeDtypeStruct((2, 8, HEAD), f32),
        in_specs=[hbm] * 3,
        out_specs=vmem,
        scratch_shapes=[
            pltpu.VMEM((TOK, D_WIN), bf16),
            pltpu.VMEM((2, TOK, HEAD), bf16),
            buffers(NX, GROUP),
            buffers(NX, GROUP),
            buffers(NX, GROUP),
            buffers(NX, GROUP),
            buffers(NX - 1, GROUP),
            buffers(GROUP, dtype=f32),
            buffers(GROUP),
            buffers(NY - 1),
            pltpu.VMEM((128, HEAD), f32),
            pltpu.VMEM((2 * NZ, 8, HEAD), f32),
            pltpu.VMEM((2 * NZ, 8, HEAD), f32),
            dma((2 + len(LOADS),)),
            dma((count,)),
            dma((count,)),
            dma((count,)),
            dma((count,)),
            dma((count,)),
            dma((count,)),
            dma,
            dma,
            pltpu.SemaphoreType.REGULAR,
            pltpu.SemaphoreType.REGULAR,
        ],
        compiler_params=pltpu.CompilerParams(
            collective_id=0, has_side_effects=True, vmem_limit_bytes=55140 * 1024
        ),
    )(x_normed, key_grad, value_grad)
    return both[0, :OWN], both[1, :OWN]


def solution(mesh):
    rows = P(("outer", "inner"), None)
    return jax.shard_map(per_device, mesh=mesh, in_specs=(rows,) * 3, out_specs=(rows, rows), check_vma=False)
```

```python
import jax
import jax.numpy as jnp
from jax import lax
from jax.experimental import pallas as pl
from jax.experimental.pallas import tpu as pltpu
from jax.sharding import PartitionSpec as P

MESH = pl.DeviceIdType.MESH
NX, NY, NZ = 4, 8, 12
D_WIN, HEAD, TOK = 3840, 128, 512
ROWS = 120
OWN = 5
LOADS = (2560, 1280)
COLS = 256
PIECES = (
    ((0, 4), 0, 16),
    ((4, 4), 0, 16),
    ((0, 4), 16, 32),
    ((0, 4), 32, 64),
    ((4, 4), 16, 48),
    ((0, 4), 64, 96),
    ((4, 4), 48, 80),
    ((0, 4), 96, 120),
    ((4, 4), 80, 120),
)
HEIGHTS = tuple(-(-(hi - lo) // 16) * 16 for _, lo, hi in PIECES)
ORDER = (
    "x0", "c1", "c2", "x1", "c3", "x2", "c4", "x3", "c5", "x4", "c6", "x5", "c7", "x6", "c8", "x7", "y0", "x8",
    "y1", "y2", "m0", "y3", "y4", "m1", "z0", "z1", "z2", "y5", "z3", "y6", "z4", "z5", "y7", "z6", "y8", "z7",
    "z8",
)
bf16, f32 = jnp.bfloat16, jnp.float32


def device(x, y, z, core):
    return ((x * NY + y) * 3 + z // 4, (z % 4) * 2 + core)


def kernel(x_hbm, k_hbm, v_hbm, out, xv, g, give, keep, got, xs, xr, yf, ys, yr, total, zs, zr, load_sem, core_send,
           core_recv, x_send, x_recv, y_send, y_recv, z_send, z_recv, plane_in, line_in):
    outer, inner = lax.axis_index("outer"), lax.axis_index("inner")
    x, y = outer // (NY * 3), (outer // 3) % NY
    z, core = (outer % 3) * 4 + inner // 2, inner % 2
    other = 1 - core

    loads = [pltpu.make_async_copy(k_hbm, g.at[0], load_sem.at[0]), pltpu.make_async_copy(v_hbm, g.at[1], load_sem.at[1])]
    segments, at = [], 0
    for n, width in enumerate(LOADS):
        segments.append((at, at + width))
        part = pl.ds(at, width)
        loads.append(pltpu.make_async_copy(x_hbm.at[:, part], xv.at[:, part], load_sem.at[2 + n]))
        at += width
    for copy in loads:
        copy.start()

    barrier = pltpu.get_barrier_semaphore()

    def signal(sem, to):
        pl.semaphore_signal(sem, inc=1, device_id=to, device_id_type=MESH)

    for d in (4, 3, 5, 2, 6, 1, 7):
        signal(barrier, device(x, (y + d) % NY, z, 0))
    for d in (2, 1, 3):
        signal(barrier, device((x + d) % NX, y, z, 0))

    @pl.when(core == 1)
    def _():
        signal(barrier, device(x, y, z, 0))

    for d in (6, 5, 7, 4, 8, 3, 9, 2, 10, 1, 11):
        signal(barrier, device(x, y, (z + d) % NZ, 1))

    def meet_plane():
        @pl.when(core == 0)
        def _():
            pl.semaphore_wait(barrier, 2 * (NX - 1) + 2 * (NY - 1) + 1)
            signal(plane_in, device(x, y, z, 1))

    loads[0].wait()
    loads[1].wait()
    gt = jnp.concatenate([g[other].T, g[core].T], axis=0)
    for n in range(D_WIN // COLS):
        start, stop = n * COLS, (n + 1) * COLS
        for m, (first, last) in enumerate(segments):
            if start == first:
                if m == len(segments) - 1:
                    meet_plane()
                loads[2 + m].wait()
        part = jnp.dot(gt, xv[:, start:stop], preferred_element_type=f32).astype(bf16)
        for half, dest in ((part[:HEAD].T, give), (part[HEAD:].T, keep)):
            for block in range(start // ROWS, -(-stop // ROWS)):
                for p, (group, lo, hi) in enumerate(PIECES):
                    first, last = max(start, block * ROWS + lo), min(stop, block * ROWS + hi)
                    if first < last and 0 <= block % NY - group[0] < group[1]:
                        at = first - block * ROWS - lo
                        dest[p][block // NY, block % NY - group[0], at : at + last - first, :] = half[first - start : last - start]


    @pl.when(core == 1)
    def _():
        pl.semaphore_wait(plane_in, 1)

    def remote(src, dst, send, recv, to):
        return pltpu.make_async_remote_copy(
            src_ref=src, dst_ref=dst, send_sem=send, recv_sem=recv, device_id=to, device_id_type=MESH
        )

    def wait(ref, sem):
        pltpu.make_async_copy(ref, ref, sem).wait()

    swaps = [
        remote(give[p], got[p], core_send.at[p], core_recv.at[p], device(x, y, z, other)) if p else None
        for p in range(len(PIECES))
    ]

    def swap_cores(p):
        swaps[p].start()

    def in_group(p):
        first, count = PIECES[p][0]
        return jnp.logical_and(y >= first, y < first + count)

    def along_x(p):
        if p == 0:
            for d in (2, 1, 3):
                to = (x + d) % NX
                remote(keep[0].at[to], xr[0].at[d - 1], x_send.at[0], x_recv.at[0], device(to, y, z, core)).start()
                remote(give[0].at[to], xr[0].at[d + 2], x_send.at[0], x_recv.at[0], device(to, y, z, other)).start()
            remote(give[0].at[x], xr[0].at[6], x_send.at[0], x_recv.at[0], device(x, y, z, other)).start()
            return
        swaps[p].wait_recv()
        for n in range(NX):
            xs[p][n] = (keep[p][n].astype(f32) + got[p][n].astype(f32)).astype(bf16)
        for d in (2, 1, 3):
            to = (x + d) % NX
            remote(xs[p].at[to], xr[p].at[d - 1], x_send.at[p], x_recv.at[p], device(to, y, z, core)).start()

    def along_y(p):
        wait(xr[p], x_recv.at[p])
        s = keep[p][x].astype(f32)
        if p > 0:
            s += got[p][x].astype(f32)
        for d in range(xr[p].shape[0]):
            s += xr[p][d].astype(f32)
        yf[p][...] = s
        ys[p][...] = s.astype(bf16)
        group = PIECES[p][0]
        for n in range(group[1]):
            to = group[0] + n

            @pl.when(y != to)
            def _():
                slot = (y - to + NY) % NY - 1
                remote(ys[p].at[n], yr[p].at[slot], y_send.at[p], y_recv.at[p], device(x, to, z, core)).start()

    def along_z(p):
        @pl.when(in_group(p))
        def _():
            wait(yr[p], y_recv.at[p])
            s = yf[p][y - PIECES[p][0][0]]
            for d in range(NY - 1):
                s += yr[p][d].astype(f32)
            _, lo, hi = PIECES[p]
            total[lo : lo + HEIGHTS[p]] = s
            for to in range(NZ):
                if not lo < (to + 1) * 2 * OWN <= hi:
                    continue
                for c in range(2):
                    n = to * 2 + c
                    zs[n, :OWN] = total[n * OWN : (n + 1) * OWN]

                    @pl.when(jnp.logical_or(z != to, core != c))
                    def _():
                        src, dst = zs.at[n, pl.ds(0, OWN)], zr.at[core * NZ + z, pl.ds(0, OWN)]
                        remote(src, dst, z_send, z_recv, device(x, y, to, c)).start()

    def meet_line(p):
        if p == 0:

            @pl.when(core == 1)
            def _():
                pl.semaphore_wait(barrier, 2 * (NZ - 1))
                signal(line_in, device(x, y, z, 0))

        else:

            @pl.when(core == 0)
            def _():
                pl.semaphore_wait(line_in, 1)

    steps = {"c": swap_cores, "x": along_x, "y": along_y, "z": along_z, "m": meet_line}
    for step in ORDER:
        steps[step[0]](int(step[1:]))

    zr[core * NZ + z, :OWN] = zs[z * 2 + core, :OWN]
    for p in range(len(PIECES)):
        if p > 0:
            swaps[p].wait_send()
        wait(xr[p], x_send.at[p])
        wait(yr[p].at[pl.ds(0, PIECES[p][0][1] - 1)], y_send.at[p])

        @pl.when(jnp.logical_not(in_group(p)))
        def _():
            wait(yr[p].at[0], y_send.at[p])

    all_but_one = zr.at[pl.ds(0, 2 * NZ - 1), pl.ds(0, OWN)]
    wait(all_but_one, z_send)
    wait(all_but_one, z_recv)
    for t in range(2):
        s = zr[t * NZ, :OWN]
        for d in range(1, NZ):
            s += zr[t * NZ + d, :OWN]
        out[t, :OWN] = s


def per_device(x_normed, key_grad, value_grad):
    hbm = pl.BlockSpec(memory_space=pl.ANY)
    vmem = pl.BlockSpec(memory_space=pltpu.VMEM)
    dma = pltpu.SemaphoreType.DMA
    count = len(PIECES)

    def buffers(*dims, dtype=bf16, owners=True):
        return [
            pltpu.VMEM((*dims, *((group[1],) if owners else ()), height, HEAD), dtype)
            for (group, _, _), height in zip(PIECES, HEIGHTS)
        ]

    both = pl.pallas_call(
        kernel,
        out_shape=jax.ShapeDtypeStruct((2, 8, HEAD), f32),
        in_specs=[hbm] * 3,
        out_specs=vmem,
        scratch_shapes=[
            pltpu.VMEM((TOK, D_WIN), bf16),
            pltpu.VMEM((2, TOK, HEAD), bf16),
            buffers(NX),
            buffers(NX),
            buffers(NX),
            buffers(NX),
            buffers(2 * NX - 1)[:1] + buffers(NX - 1)[1:],
            buffers(dtype=f32),
            buffers(),
            buffers(NY - 1, owners=False),
            pltpu.VMEM((128, HEAD), f32),
            pltpu.VMEM((2 * NZ, 8, HEAD), f32),
            pltpu.VMEM((2 * NZ, 8, HEAD), f32),
            dma((2 + len(LOADS),)),
            dma((count,)),
            dma((count,)),
            dma((count,)),
            dma((count,)),
            dma((count,)),
            dma((count,)),
            dma,
            dma,
            pltpu.SemaphoreType.REGULAR,
            pltpu.SemaphoreType.REGULAR,
        ],
        compiler_params=pltpu.CompilerParams(
            collective_id=0, has_side_effects=True, vmem_limit_bytes=55140 * 1024
        ),
    )(x_normed, key_grad, value_grad)
    return both[0, :OWN], both[1, :OWN]


def solution(mesh):
    rows = P(("outer", "inner"), None)
    return jax.shard_map(per_device, mesh=mesh, in_specs=(rows,) * 3, out_specs=(rows, rows), check_vma=False)
```

```python
import jax
import jax.numpy as jnp
from jax import lax
from jax.experimental import pallas as pl
from jax.experimental.pallas import tpu as pltpu
from jax.sharding import PartitionSpec as P

MESH = pl.DeviceIdType.MESH
NX, NY, NZ = 4, 8, 12
D_WIN, HEAD, TOK = 3840, 128, 512
ROWS = 120
OWN = 5
LOADS = (2560, 1280)
COLS = 256
PIECES = (
    ((0, 4), 0, 16),
    ((4, 4), 0, 16),
    ((0, 4), 16, 32),
    ((0, 4), 32, 64),
    ((4, 4), 16, 48),
    ((0, 4), 64, 96),
    ((4, 4), 48, 80),
    ((0, 4), 96, 120),
    ((4, 4), 80, 120),
)
HEIGHTS = tuple(-(-(hi - lo) // 16) * 16 for _, lo, hi in PIECES)
ORDER = (
    "x0", "c1", "c2", "c3", "c4", "c5", "c6", "c7", "c8", "x1", "x2", "x3", "x4", "x5", "x6", "x7", "y0", "x8",
    "y1", "y2", "m0", "y3", "y4", "m1", "z0", "z1", "z2", "y5", "z3", "y6", "z4", "z5", "y7", "z6", "y8", "z7",
    "z8",
)
bf16, f32 = jnp.bfloat16, jnp.float32


def device(x, y, z, core):
    return ((x * NY + y) * 3 + z // 4, (z % 4) * 2 + core)


def kernel(x_hbm, k_hbm, v_hbm, out, xv, g, give, keep, got, xs, xr, yf, ys, yr, total, zs, zr, load_sem, core_send,
           core_recv, x_send, x_recv, y_send, y_recv, z_send, z_recv, plane_in, line_in):
    outer, inner = lax.axis_index("outer"), lax.axis_index("inner")
    x, y = outer // (NY * 3), (outer // 3) % NY
    z, core = (outer % 3) * 4 + inner // 2, inner % 2
    other = 1 - core

    loads = [pltpu.make_async_copy(k_hbm, g.at[0], load_sem.at[0]), pltpu.make_async_copy(v_hbm, g.at[1], load_sem.at[1])]
    segments, at = [], 0
    for n, width in enumerate(LOADS):
        segments.append((at, at + width))
        part = pl.ds(at, width)
        loads.append(pltpu.make_async_copy(x_hbm.at[:, part], xv.at[:, part], load_sem.at[2 + n]))
        at += width
    for copy in loads:
        copy.start()

    barrier = pltpu.get_barrier_semaphore()

    def signal(sem, to):
        pl.semaphore_signal(sem, inc=1, device_id=to, device_id_type=MESH)

    for d in (4, 3, 5, 2, 6, 1, 7):
        signal(barrier, device(x, (y + d) % NY, z, 0))
    for d in (2, 1, 3):
        signal(barrier, device((x + d) % NX, y, z, 0))

    @pl.when(core == 1)
    def _():
        signal(barrier, device(x, y, z, 0))

    for d in (6, 5, 7, 4, 8, 3, 9, 2, 10, 1, 11):
        signal(barrier, device(x, y, (z + d) % NZ, 1))

    def meet_plane():
        @pl.when(core == 0)
        def _():
            pl.semaphore_wait(barrier, 2 * (NX - 1) + 2 * (NY - 1) + 1)
            signal(plane_in, device(x, y, z, 1))

    loads[0].wait()
    loads[1].wait()
    gt = jnp.concatenate([g[other].T, g[core].T], axis=0)
    for n in range(D_WIN // COLS):
        start, stop = n * COLS, (n + 1) * COLS
        for m, (first, last) in enumerate(segments):
            if start == first:
                if m == len(segments) - 1:
                    meet_plane()
                loads[2 + m].wait()
        part = jnp.dot(gt, xv[:, start:stop], preferred_element_type=f32).astype(bf16)
        for half, dest in ((part[:HEAD].T, give), (part[HEAD:].T, keep)):
            for block in range(start // ROWS, -(-stop // ROWS)):
                for p, (group, lo, hi) in enumerate(PIECES):
                    first, last = max(start, block * ROWS + lo), min(stop, block * ROWS + hi)
                    if first < last and 0 <= block % NY - group[0] < group[1]:
                        at = first - block * ROWS - lo
                        dest[p][block // NY, block % NY - group[0], at : at + last - first, :] = half[first - start : last - start]


    @pl.when(core == 1)
    def _():
        pl.semaphore_wait(plane_in, 1)

    def remote(src, dst, send, recv, to):
        return pltpu.make_async_remote_copy(
            src_ref=src, dst_ref=dst, send_sem=send, recv_sem=recv, device_id=to, device_id_type=MESH
        )

    def wait(ref, sem):
        pltpu.make_async_copy(ref, ref, sem).wait()

    swaps = [
        remote(give[p], got[p], core_send.at[p], core_recv.at[p], device(x, y, z, other)) if p else None
        for p in range(len(PIECES))
    ]

    def swap_cores(p):
        swaps[p].start()

    def in_group(p):
        first, count = PIECES[p][0]
        return jnp.logical_and(y >= first, y < first + count)

    def along_x(p):
        if p == 0:
            for d in (2, 1, 3):
                to = (x + d) % NX
                remote(keep[0].at[to], xr[0].at[d - 1], x_send.at[0], x_recv.at[0], device(to, y, z, core)).start()
                remote(give[0].at[to], xr[0].at[d + 2], x_send.at[0], x_recv.at[0], device(to, y, z, other)).start()
            remote(give[0].at[x], xr[0].at[6], x_send.at[0], x_recv.at[0], device(x, y, z, other)).start()
            return
        swaps[p].wait_recv()
        for n in range(NX):
            xs[p][n] = (keep[p][n].astype(f32) + got[p][n].astype(f32)).astype(bf16)
        for d in (2, 1, 3):
            to = (x + d) % NX
            remote(xs[p].at[to], xr[p].at[d - 1], x_send.at[p], x_recv.at[p], device(to, y, z, core)).start()

    def along_y(p):
        wait(xr[p], x_recv.at[p])
        s = keep[p][x].astype(f32)
        if p > 0:
            s += got[p][x].astype(f32)
        for d in range(xr[p].shape[0]):
            s += xr[p][d].astype(f32)
        yf[p][...] = s
        ys[p][...] = s.astype(bf16)
        group = PIECES[p][0]
        for n in range(group[1]):
            to = group[0] + n

            @pl.when(y != to)
            def _():
                slot = (y - to + NY) % NY - 1
                remote(ys[p].at[n], yr[p].at[slot], y_send.at[p], y_recv.at[p], device(x, to, z, core)).start()

    def along_z(p):
        @pl.when(in_group(p))
        def _():
            wait(yr[p], y_recv.at[p])
            s = yf[p][y - PIECES[p][0][0]]
            for d in range(NY - 1):
                s += yr[p][d].astype(f32)
            _, lo, hi = PIECES[p]
            total[lo : lo + HEIGHTS[p]] = s
            for to in range(NZ):
                if not lo < (to + 1) * 2 * OWN <= hi:
                    continue
                for c in range(2):
                    n = to * 2 + c
                    zs[n, :OWN] = total[n * OWN : (n + 1) * OWN]

                    @pl.when(jnp.logical_or(z != to, core != c))
                    def _():
                        src, dst = zs.at[n, pl.ds(0, OWN)], zr.at[core * NZ + z, pl.ds(0, OWN)]
                        remote(src, dst, z_send, z_recv, device(x, y, to, c)).start()

    def meet_line(p):
        if p == 0:

            @pl.when(core == 1)
            def _():
                pl.semaphore_wait(barrier, 2 * (NZ - 1))
                signal(line_in, device(x, y, z, 0))

        else:

            @pl.when(core == 0)
            def _():
                pl.semaphore_wait(line_in, 1)

    steps = {"c": swap_cores, "x": along_x, "y": along_y, "z": along_z, "m": meet_line}
    for step in ORDER:
        steps[step[0]](int(step[1:]))

    zr[core * NZ + z, :OWN] = zs[z * 2 + core, :OWN]
    for p in range(len(PIECES)):
        if p > 0:
            swaps[p].wait_send()
        wait(xr[p], x_send.at[p])
        wait(yr[p].at[pl.ds(0, PIECES[p][0][1] - 1)], y_send.at[p])

        @pl.when(jnp.logical_not(in_group(p)))
        def _():
            wait(yr[p].at[0], y_send.at[p])

    all_but_one = zr.at[pl.ds(0, 2 * NZ - 1), pl.ds(0, OWN)]
    wait(all_but_one, z_send)
    wait(all_but_one, z_recv)
    for t in range(2):
        s = zr[t * NZ, :OWN]
        for d in range(1, NZ):
            s += zr[t * NZ + d, :OWN]
        out[t, :OWN] = s


def per_device(x_normed, key_grad, value_grad):
    hbm = pl.BlockSpec(memory_space=pl.ANY)
    vmem = pl.BlockSpec(memory_space=pltpu.VMEM)
    dma = pltpu.SemaphoreType.DMA
    count = len(PIECES)

    def buffers(*dims, dtype=bf16, owners=True):
        return [
            pltpu.VMEM((*dims, *((group[1],) if owners else ()), height, HEAD), dtype)
            for (group, _, _), height in zip(PIECES, HEIGHTS)
        ]

    both = pl.pallas_call(
        kernel,
        out_shape=jax.ShapeDtypeStruct((2, 8, HEAD), f32),
        in_specs=[hbm] * 3,
        out_specs=vmem,
        scratch_shapes=[
            pltpu.VMEM((TOK, D_WIN), bf16),
            pltpu.VMEM((2, TOK, HEAD), bf16),
            buffers(NX),
            buffers(NX),
            buffers(NX),
            buffers(NX),
            buffers(2 * NX - 1)[:1] + buffers(NX - 1)[1:],
            buffers(dtype=f32),
            buffers(),
            buffers(NY - 1, owners=False),
            pltpu.VMEM((128, HEAD), f32),
            pltpu.VMEM((2 * NZ, 8, HEAD), f32),
            pltpu.VMEM((2 * NZ, 8, HEAD), f32),
            dma((2 + len(LOADS),)),
            dma((count,)),
            dma((count,)),
            dma((count,)),
            dma((count,)),
            dma((count,)),
            dma((count,)),
            dma,
            dma,
            pltpu.SemaphoreType.REGULAR,
            pltpu.SemaphoreType.REGULAR,
        ],
        compiler_params=pltpu.CompilerParams(
            collective_id=0, has_side_effects=True, vmem_limit_bytes=55140 * 1024
        ),
    )(x_normed, key_grad, value_grad)
    return both[0, :OWN], both[1, :OWN]


def solution(mesh):
    rows = P(("outer", "inner"), None)
    return jax.shard_map(per_device, mesh=mesh, in_specs=(rows,) * 3, out_specs=(rows, rows), check_vma=False)
```
